512 devices in a mesh: seq: 256 (over x, y, z), batch: 2 (over core).
Axes of the slice: x: 4, y: 8, z: 8, core: 2. Of those that a mesh axis runs over, the one named last changes fastest.
Arguments:
- query_in: bfloat16 [262144, 1024], P(('batch', 'seq')), parts along dimension 0, may hold values from -6 to 6
- key_in: bfloat16 [262144, 1024], P(('batch', 'seq')), parts along dimension 0, may hold values from -6 to 6
- value_in: bfloat16 [262144, 1024], P(('batch', 'seq')), parts along dimension 0, may hold values from -6 to 6
- conv_weight: float32 [3, 4, 1024], replicated, may hold values from -3 to 3
- level_weights: float32 [5, 8, 262144], P(None, None, ('batch', 'seq')), parts along dimension 2, may hold values from 0.1 to 1
- out_gain: float32 [1024], replicated, may hold values from 0.25 to 1.75
Outputs:
- mixed_out: bfloat16 [262144, 1024], P(('batch', 'seq')), parts along dimension 0
The draws below stay inside these ranges and needn't reach their ends.
There are 2 independent parts, one for each index of `batch`. The reference program is written for one: setup_inputs(seed, part) draws one part's arguments, and reference() takes and returns one part's arrays. A program takes and returns all parts, laid end to end along the dimension named above; an argument that names none is the same for every part. Nothing has to cross between parts.
All inputs are finite; a program needn't handle non-finite values.
Results may differ from the reference program's by a relative error of at most 0.005.
Values may be sent and summed in bfloat16 or wider, within the bound.
A program may use at most 64 MiB of HBM per device.

```python
import math
import jax
import jax.numpy as jnp
from jax import lax

HEADS = 8
DK = 128
D = 1024
TAPS = 4
LEVELS = 4
TOK_DEV = 512
RADIX = 4
TOKENS = 131072
N_SEQ = 256


def shard_levels(stream_key, dims, shards, low, high):
    level, own = 1.0, jax.random.fold_in(stream_key, 6)
    for dim, shards_of in shards:
        steps = jnp.exp(jax.random.uniform(jax.random.fold_in(own, dim), (shards_of,), jnp.float32, low / len(shards), high / len(shards)))
        level = level * jnp.repeat(steps, dims[dim] // shards_of).reshape([-1 if axis == dim else 1 for axis in range(len(dims))])
    return level


def normal_values(stream_key, shape, scale, reach, cuts=(), kind=jnp.bfloat16):
    drawn = jax.random.normal(stream_key, shape, jnp.float32) * scale
    if len(cuts) > 0:
        drawn = shard_levels(stream_key, shape, cuts, -0.22, 0.18) * drawn
    return jnp.clip(drawn, min=-reach, max=reach).astype(kind)


def setup_inputs(seed: int = 0, part: int = 0) -> dict:
    splits = jax.random.split(jax.random.key(seed), 7)
    own_keys = jax.random.split(jax.random.fold_in(splits[6], part), 7)
    return {
        "query_in": normal_values(own_keys[0], (TOKENS, D), 1.0, 6.0, ((0, 256),)),
        "key_in": normal_values(own_keys[1], (TOKENS, D), 1.0, 6.0, ((0, 256),)),
        "value_in": normal_values(own_keys[2], (TOKENS, D), 1.0, 6.0, ((0, 256),)),
        "conv_weight": normal_values(splits[3], (3, TAPS, D), TAPS ** -0.5, 3.0, (), jnp.float32),
        "level_weights": jnp.clip(jnp.exp(math.log(1.0) - 2.3025851 * jax.random.uniform(own_keys[4], (LEVELS + 1, HEADS, TOKENS), jnp.float32) ** shard_levels(own_keys[4], (LEVELS + 1, HEADS, TOKENS), ((2, 256),), -0.2, 0.2)), 0.1, 1.0),
        "out_gain": jnp.clip(1.0 + 0.15 * jax.random.normal(splits[5], (D,), jnp.float32), 0.25, 1.75),
    }


EPS = 1e-06

def short_conv(stream, kernel):
    values = stream.astype(jnp.float32)
    tap_count = kernel.shape[0]
    padded = jnp.pad(values, ((tap_count - 1, 0), (0, 0)))
    summed = jnp.zeros_like(values)
    for offset in range(tap_count):
        summed = summed + kernel[offset] * padded[offset:offset + values.shape[0]]
    return jax.nn.silu(summed)

def unit_heads(values):
    shaped = values.reshape(values.shape[0], HEADS, DK)
    return (shaped / jnp.sqrt(lax.optimization_barrier(jnp.sum(shaped * shaped, axis=-1, keepdims=True)) + EPS)).astype(jnp.bfloat16)

def reference(query_in, key_in, value_in, conv_weight, level_weights, out_gain):
    queries = unit_heads(short_conv(query_in, conv_weight[0]))
    keys = unit_heads(short_conv(key_in, conv_weight[1]))
    values = short_conv(value_in, conv_weight[2]).reshape(TOKENS, HEADS, DK).astype(jnp.bfloat16)
    span_count = N_SEQ
    query_spans = queries.reshape(span_count, TOK_DEV, HEADS, DK)
    key_spans = keys.reshape(span_count, TOK_DEV, HEADS, DK)
    value_spans = values.reshape(span_count, TOK_DEV, HEADS, DK)

    def span_state(pair):
        return jnp.einsum('chd,che->hde', pair[0].astype(jnp.float32), pair[1].astype(jnp.float32))
    states = lax.map(span_state, (key_spans, value_spans))
    span_ids = jnp.arange(span_count, dtype=jnp.int32)
    level_list = []
    scale_list = []
    for level_index in range(LEVELS):
        child = RADIX ** level_index
        parent = RADIX ** (level_index + 1)
        blocks = states.reshape(span_count // parent, RADIX, child, HEADS, DK, DK).sum(axis=2)
        running = jnp.cumsum(blocks, axis=1)
        earlier_sum = jnp.concatenate([jnp.zeros_like(blocks[:, :1]), running[:, :-1]], axis=1)
        level_list.append(jnp.repeat(earlier_sum, child, axis=1).reshape(span_count, HEADS, DK, DK))
        tokens_before = TOK_DEV * (span_ids % parent - span_ids % child)
        scale_list.append(1.0 / jnp.sqrt(jnp.maximum(tokens_before, 1).astype(jnp.float32)))
    buckets = jnp.stack(level_list, axis=1)
    scales = jnp.stack(scale_list, axis=1)
    mixing = level_weights.reshape(LEVELS + 1, HEADS, span_count, TOK_DEV).transpose(2, 0, 3, 1)

    def one_span(items):
        query, key, value, weights_here, bucket, scale = items
        positions = jnp.arange(TOK_DEV)
        scores = jnp.einsum('thd,shd->hts', query.astype(jnp.float32), key.astype(jnp.float32))
        causal_mask = (positions[None, :] <= positions[:, None]).astype(jnp.float32)
        weights = (scores * causal_mask / jnp.sqrt(positions + 1.0)[:, None]).astype(jnp.bfloat16)
        local_mix = jnp.einsum('hts,shd->thd', weights.astype(jnp.float32), value.astype(jnp.float32))
        mixed = weights_here[0][:, :, None] * local_mix
        query_wide = query.astype(jnp.float32)
        for level_index in range(LEVELS):
            projected = jnp.einsum('thd,hde->the', query_wide, bucket[level_index], precision=lax.Precision.HIGHEST)
            mixed = mixed + (weights_here[level_index + 1] * scale[level_index])[:, :, None] * projected
        normed = mixed / jnp.sqrt(lax.optimization_barrier(jnp.mean(mixed * mixed, axis=-1, keepdims=True)) + EPS) * out_gain.reshape(HEADS, DK)
        return normed.astype(jnp.bfloat16).reshape(TOK_DEV, D)
    outputs = lax.map(one_span, (query_spans, key_spans, value_spans, mixing, buckets, scales))
    return outputs.reshape(TOKENS, D)
```

```python
import functools

import jax
import jax.numpy as jnp
from jax import lax
from jax.experimental import pallas as pl
from jax.experimental.pallas import tpu as pltpu
from jax.sharding import PartitionSpec as P

MESH = pl.DeviceIdType.MESH
EPS = 1e-6
H = 8
DK = 128
T = 512
NX, NY, NZ = 4, 8, 8
F32 = jnp.float32
BF16 = jnp.bfloat16


def level_factor(digit, level):
    base = (1.0 / (T * 4.0**level)) ** 0.5
    return jnp.where(
        digit == 0, 0.0, jnp.where(digit == 1, base, jnp.where(digit == 2, base * 0.5**0.5, base * (1.0 / 3.0) ** 0.5))
    )


def kernel(
    q_hbm, k_hbm, v_hbm, cw_ref, lw_ref, gain_ref, out_hbm,
    xin, tails, halo_f, halo_send, halo_recv, xf, xfs, qs, ks, vs, lwh, acc,
    state, a_recv, b0_send, b1_send, yr, xt, buckets, obuf, own_f,
    in_sem, tail_sem, out_sem, halo_sem, a_ss, a_rs, y_ss, y_rs, x_ss, x_rs, b_ss, b_rs,
):
    me = lax.axis_index("seq")
    core = lax.axis_index("batch")
    x, y, z = me // 64, lax.rem(me // 8, 8), lax.rem(me, 8)

    def dev(xx, yy, zz):
        return (xx * 64 + yy * 8 + zz, core)

    ins = (q_hbm, k_hbm, v_hbm)

    def head_of(step):
        return lax.rem(z + 1 + step, NZ)

    def load(stream, head):
        cols = pl.ds(pl.multiple_of(head * DK, DK), DK)
        return pltpu.make_async_copy(ins[stream].at[:, cols], xin.at[stream, head], in_sem.at[stream, head])

    def tail(stream):
        return pltpu.make_async_copy(ins[stream].at[pl.ds(T - 16, 16), :], tails.at[stream], tail_sem.at[stream])

    for stream in range(3):
        tail(stream).start()

    def start_loads(step, carry):
        for stream in (1, 2):
            load(stream, head_of(step)).start()
        return carry

    lax.fori_loop(0, H, start_loads, 0)

    def start_q(head, carry):
        load(0, head).start()
        return carry

    lax.fori_loop(0, H, start_q, 0)

    barrier = pltpu.get_barrier_semaphore()

    def greet_ring(step, carry):
        pl.semaphore_signal(barrier, inc=1, device_id=dev(x, y, lax.rem(z + step, NZ)), device_id_type=MESH)
        pl.semaphore_signal(barrier, inc=1, device_id=dev(x, lax.rem(y + step, NY), z), device_id_type=MESH)
        return carry

    lax.fori_loop(1, NZ, greet_ring, 0)
    for step in range(1, NX):
        pl.semaphore_signal(barrier, inc=1, device_id=dev(lax.rem(x + step, NX), y, z), device_id_type=MESH)
    pl.semaphore_signal(barrier, inc=1, device_id=(lax.rem(me + 255, 256), core), device_id_type=MESH)

    halo_f[...] = jnp.zeros_like(halo_f)
    for stream in range(3):
        tail(stream).wait()
        halo_f[pl.ds(3 * stream, 3), :] = tails[stream].astype(F32)[13:16, :]
    halo_send[...] = halo_f[...].astype(BF16)
    halo = pltpu.make_async_remote_copy(
        halo_send, halo_recv, halo_sem.at[0], halo_sem.at[1], device_id=(lax.rem(me + 1, 256), core), device_id_type=MESH
    )

    pl.semaphore_wait(barrier, 18)
    halo.start()

    lw = jnp.concatenate([lw_ref[...], jnp.zeros((128 - 5 * H, T), F32)], axis=0).T
    pos = lax.broadcasted_iota(jnp.int32, (T, 128), 0).astype(F32)
    lane = lax.broadcasted_iota(jnp.int32, (T, 128), 1)
    lw = jnp.where(lane < H, lw * lax.rsqrt(pos + 1.0), lw)
    for head in range(H):
        lwh[head] = lw if head == 0 else pltpu.roll(lw, 128 - head, 1)

    ones = jnp.ones((DK, DK), BF16)

    def taps(stream, head):
        cols = pl.ds(pl.multiple_of(head * DK, DK), DK)
        return [cw_ref[stream, pl.ds(j, 1), cols] for j in range(4)]

    def silu(c):
        return c * pl.reciprocal(1.0 + jnp.exp(-c), approx=True)

    def unit(a):
        total = jnp.dot((a * a).astype(BF16), ones, preferred_element_type=F32)
        return a * lax.rsqrt(total + EPS)

    def conv_rows(src, w, row, count):
        c = w[0] * src[pl.ds(row + 5, count), :]
        for j in range(1, 4):
            c = c + w[j] * src[pl.ds(row + 5 + j, count), :]
        return silu(c)

    CH = 128

    def stream_head(stream, head, dst, halo_rows):
        w = taps(stream, head)
        buf = xf.at[stream]
        if halo_rows is None:
            buf[pl.ds(0, 8), :] = jnp.zeros((8, DK), F32)
        else:
            buf[pl.ds(5, 3), :] = halo_rows
        buf[pl.ds(8, T), :] = xin[stream, head].astype(F32)
        for row in range(0, T, CH):
            a = conv_rows(buf, w, row, CH)
            if stream < 2:
                a = unit(a)
            dst[head, pl.ds(row, CH), :] = a.astype(BF16)

    def kv_step(step, carry):
        head = head_of(step)
        for stream, dst in ((1, ks), (2, vs)):
            load(stream, head).wait()
            stream_head(stream, head, dst, None)
        return carry

    lax.fori_loop(0, H, kv_step, 0)

    halo.wait()
    halo_f[...] = jnp.where(me == 0, 0.0, halo_recv[...].astype(F32))

    def halo_rows(stream, head):
        cols = pl.ds(pl.multiple_of(head * DK, DK), DK)
        return halo_f[pl.ds(3 * stream, 3), cols]

    def to_owner(head):
        return pltpu.make_async_remote_copy(
            state.at[head], a_recv.at[z], a_ss.at[head], a_rs.at[z], device_id=dev(x, y, head), device_id_type=MESH
        )

    def from_row(source):
        return pltpu.make_async_remote_copy(
            state.at[source], a_recv.at[source], a_ss.at[source], a_rs.at[source],
            device_id=dev(x, y, source), device_id_type=MESH,
        )

    def state_of(head):
        for stream, dst in ((1, ks), (2, vs)):
            xfs[pl.ds(5, 3), :] = halo_rows(stream, head)
            xfs[pl.ds(8, 16), :] = xin[stream, head, pl.ds(0, 16), :].astype(F32)
            a = conv_rows(xfs, taps(stream, head), 0, 16)
            if stream == 1:
                a = unit(a)
            dst[head, pl.ds(0, 16), :] = a.astype(BF16)
        return lax.dot_general(ks[head], vs[head], (((0,), (0,)), ((), ())), preferred_element_type=F32)

    def state_step(step, carry):
        head = head_of(step)
        state[head] = state_of(head).astype(BF16)
        to_owner(head).start()
        return carry

    lax.fori_loop(0, H - 1, state_step, 0)
    a_recv[z] = state_of(z).astype(BF16)

    row_i = lax.broadcasted_iota(jnp.int32, (256, 256), 0)
    col_i = lax.broadcasted_iota(jnp.int32, (256, 256), 1)
    causal = row_i >= col_i
    NT = (((1,), (1,)), ((), ()))

    def weight(head, level):
        return jnp.broadcast_to(lwh[head, :, pl.ds(8 * level, 1)], (T, DK))

    def local_step(head, carry):
        load(0, head).wait()
        stream_head(0, head, qs, halo_rows(0, head))
        q0, q1 = qs[head, pl.ds(0, 256), :], qs[head, pl.ds(256, 256), :]
        k0, k1 = ks[head, pl.ds(0, 256), :], ks[head, pl.ds(256, 256), :]
        v0, v1 = vs[head, pl.ds(0, 256), :], vs[head, pl.ds(256, 256), :]
        s00 = jnp.where(causal, lax.dot_general(q0, k0, NT, preferred_element_type=F32), 0.0).astype(BF16)
        s10 = lax.dot_general(q1, k0, NT, preferred_element_type=F32).astype(BF16)
        s11 = jnp.where(causal, lax.dot_general(q1, k1, NT, preferred_element_type=F32), 0.0).astype(BF16)
        o0 = jnp.dot(s00, v0, preferred_element_type=F32)
        o1 = jnp.dot(s10, v0, preferred_element_type=F32) + jnp.dot(s11, v1, preferred_element_type=F32)
        w = weight(head, 0)
        acc[head, pl.ds(0, 256), :] = w[:256] * o0
        acc[head, pl.ds(256, 256), :] = w[256:] * o1
        return carry

    lax.fori_loop(0, H, local_step, 0)

    def wait_row(step, carry):
        from_row(lax.rem(z + step, NZ)).wait_recv()
        return carry

    lax.fori_loop(1, NZ, wait_row, 0)
    own_lo = None
    row_sum = None
    for zz in range(NZ):
        s = a_recv[zz].astype(F32)
        if zz % 4 == 0:
            b0_send[zz] = jnp.zeros((DK, DK), BF16)
            group = s
        else:
            b0_send[zz] = (group * ((1.0 / (T * (zz % 4))) ** 0.5)).astype(BF16)
            group = group + s
        if zz == 3:
            own_lo = group
        if zz == 7:
            row_sum = own_lo + group
    own_f[0] = own_lo
    yr[y] = row_sum.astype(BF16)

    def row_copy(src_y, dst_y, sem_y):
        return pltpu.make_async_remote_copy(
            yr.at[src_y], yr.at[src_y], y_ss.at[dst_y], y_rs.at[src_y], device_id=dev(x, dst_y, z), device_id_type=MESH
        )

    def send_rows(step, carry):
        to = lax.rem(y + step, NY)
        row_copy(y, to, y).start()
        return carry

    lax.fori_loop(1, NY, send_rows, 0)

    def bucket_copy(level, src, to, head):
        return pltpu.make_async_remote_copy(
            src, buckets.at[level, head], b_ss.at[level, to], b_rs.at[level, head], device_id=dev(x, y, to), device_id_type=MESH
        )

    def send_b0(step, carry):
        to = lax.rem(z + step, NZ)
        bucket_copy(0, b0_send.at[to], to, z).start()
        return carry

    lax.fori_loop(1, NZ, send_b0, 0)
    buckets[0, z] = b0_send[z]

    def wait_rows(step, carry):
        src = lax.rem(y + step, NY)
        row_copy(src, src, src).wait_recv()
        return carry

    lax.fori_loop(1, NY, wait_rows, 0)

    odd = lax.rem(y, 2)
    pair = y // 2
    before = jnp.where(odd == 1, 1.0, 0.0) * yr[jnp.maximum(y - 1, 0)].astype(F32)
    b1_send[0] = (level_factor(2 * odd, 1) * before).astype(BF16)
    b1_send[1] = (level_factor(2 * odd + 1, 1) * (before + own_f[0])).astype(BF16)
    earlier = jnp.zeros((DK, DK), F32)
    plane = jnp.zeros((DK, DK), F32)
    for yy in range(NY):
        r = yr[yy].astype(F32)
        plane = plane + r
        earlier = earlier + jnp.where(yy < 2 * pair, 1.0, 0.0) * r
    b1_send[2] = (level_factor(pair, 2) * earlier).astype(BF16)
    xt[x] = plane.astype(BF16)

    def plane_copy(src_x, dst_x):
        return pltpu.make_async_remote_copy(
            xt.at[src_x], xt.at[src_x], x_ss.at[dst_x], x_rs.at[src_x], device_id=dev(dst_x, y, z), device_id_type=MESH
        )

    for step in range(1, NX):
        plane_copy(x, lax.rem(x + step, NX)).start()

    def send_b12(step, carry):
        to = lax.rem(z + step, NZ)
        bucket_copy(1, b1_send.at[to // 4], to, z).start()
        return carry

    lax.fori_loop(1, NZ, send_b12, 0)

    def send_b2(step, carry):
        to = lax.rem(z + step, NZ)
        bucket_copy(2, b1_send.at[2], to, z).start()
        return carry

    lax.fori_loop(1, NZ, send_b2, 0)
    buckets[1, z] = b1_send[z // 4]
    buckets[2, z] = b1_send[2]

    def wait_bucket(level, head):
        @pl.when(head != z)
        def _():
            bucket_copy(level, b1_send.at[2], head, head).wait_recv()

    def project(level, head):
        return weight(head, level + 1) * jnp.dot(qs[head], buckets[level, head], preferred_element_type=F32)

    def add_level(level):
        def step(i, carry):
            head = lax.rem(z + i, NZ)
            wait_bucket(level, head)
            acc[head] += project(level, head)
            return carry

        lax.fori_loop(0, H, step, 0)

    for step in range(1, NX):
        src = lax.rem(x + step, NX)
        plane_copy(src, src).wait_recv()
    earlier = jnp.zeros((DK, DK), F32)
    for xx in range(NX):
        earlier = earlier + jnp.where(xx < x, 1.0, 0.0) * xt[xx].astype(F32)
    b1_send[3] = (level_factor(x, 3) * earlier).astype(BF16)

    def send_b3(step, carry):
        to = lax.rem(z + step, NZ)
        bucket_copy(3, b1_send.at[3], to, z).start()
        return carry

    lax.fori_loop(1, NZ, send_b3, 0)
    buckets[3, z] = b1_send[3]

    add_level(0)
    add_level(1)
    add_level(2)

    def store(head):
        cols = pl.ds(pl.multiple_of(head * DK, DK), DK)
        return pltpu.make_async_copy(obuf.at[head], out_hbm.at[:, cols], out_sem.at[head])

    def last_step(i, carry):
        head = lax.rem(z + i, NZ)
        wait_bucket(3, head)
        mixed = acc[head] + project(3, head)
        total = jnp.dot((mixed * mixed).astype(BF16), ones, preferred_element_type=F32)
        cols = pl.ds(pl.multiple_of(head * DK, DK), DK)
        obuf[head] = (mixed * lax.rsqrt(total * (1.0 / DK) + EPS) * gain_ref[:, cols]).astype(BF16)
        store(head).start()
        return carry

    lax.fori_loop(0, H, last_step, 0)

    def drain(step, carry):
        to = lax.rem(z + step, NZ)
        from_row(to).wait_send()
        ty = lax.rem(y + step, NY)
        row_copy(y, ty, y).wait_send()
        for level in range(4):
            bucket_copy(level, b1_send.at[2], to, z).wait_send()
        return carry

    lax.fori_loop(1, NZ, drain, 0)
    for step in range(1, NX):
        plane_copy(x, lax.rem(x + step, NX)).wait_send()

    def stored(head, carry):
        store(head).wait()
        return carry

    lax.fori_loop(0, H, stored, 0)


def shards(query_in, key_in, value_in, conv_weight, level_weights, out_gain):
    anywhere = pl.BlockSpec(memory_space=pl.ANY)
    vmem = pl.BlockSpec(memory_space=pltpu.VMEM)
    dma = pltpu.SemaphoreType.DMA
    return pl.pallas_call(
        kernel,
        out_shape=jax.ShapeDtypeStruct((T, H * DK), BF16),
        in_specs=[anywhere] * 3 + [vmem] * 3,
        out_specs=anywhere,
        scratch_shapes=[
            pltpu.VMEM((3, H, T, DK), BF16),
            pltpu.VMEM((3, 16, H * DK), BF16),
            pltpu.VMEM((16, H * DK), F32),
            pltpu.VMEM((16, H * DK), BF16),
            pltpu.VMEM((16, H * DK), BF16),
            pltpu.VMEM((3, T + 8, DK), F32),
            pltpu.VMEM((24, DK), F32),
            pltpu.VMEM((H, T, DK), BF16),
            pltpu.VMEM((H, T, DK), BF16),
            pltpu.VMEM((H, T, DK), BF16),
            pltpu.VMEM((H, T, DK), F32),
            pltpu.VMEM((H, T, DK), F32),
            pltpu.VMEM((H, DK, DK), BF16),
            pltpu.VMEM((NZ, DK, DK), BF16),
            pltpu.VMEM((NZ, DK, DK), BF16),
            pltpu.VMEM((4, DK, DK), BF16),
            pltpu.VMEM((NY, DK, DK), BF16),
            pltpu.VMEM((NX, DK, DK), BF16),
            pltpu.VMEM((4, H, DK, DK), BF16),
            pltpu.VMEM((H, T, DK), BF16),
            pltpu.VMEM((1, DK, DK), F32),
            dma((3, H)),
            dma((3,)),
            dma((H,)),
            dma((2,)),
            dma((NZ,)),
            dma((NZ,)),
            dma((NY,)),
            dma((NY,)),
            dma((NX,)),
            dma((NX,)),
            dma((4, NZ)),
            dma((4, NZ)),
        ],
        compiler_params=pltpu.CompilerParams(
            collective_id=0, has_side_effects=True, vmem_limit_bytes=48 * 1024 * 1024
        ),
        cost_estimate=pl.CostEstimate(flops=2 * 10**9, bytes_accessed=4 * 2**20, transcendentals=2 * 10**6),
    )(query_in, key_in, value_in, conv_weight, level_weights.reshape(5 * H, T), out_gain.reshape(1, H * DK))


def solution(mesh):
    return jax.shard_map(
        shards,
        mesh=mesh,
        in_specs=(
            P(("batch", "seq"), None),
            P(("batch", "seq"), None),
            P(("batch", "seq"), None),
            P(),
            P(None, None, ("batch", "seq")),
            P(),
        ),
        out_specs=P(("batch", "seq"), None),
        check_vma=False,
    )
```

```python
import functools

import jax
import jax.numpy as jnp
from jax import lax
from jax.experimental import pallas as pl
from jax.experimental.pallas import tpu as pltpu
from jax.sharding import PartitionSpec as P

MESH = pl.DeviceIdType.MESH
EPS = 1e-6
H = 8
DK = 128
T = 512
NX, NY, NZ = 4, 8, 8
F32 = jnp.float32
BF16 = jnp.bfloat16


def level_factor(digit, level):
    base = (1.0 / (T * 4.0**level)) ** 0.5
    return jnp.where(
        digit == 0, 0.0, jnp.where(digit == 1, base, jnp.where(digit == 2, base * 0.5**0.5, base * (1.0 / 3.0) ** 0.5))
    )


def kernel(
    q_hbm, k_hbm, v_hbm, cw_hbm, lw_hbm, gain_hbm, out_hbm,
    cw_ref, lw_ref, gain_ref,
    xin, tails, halo_f, halo_send, halo_recv, xf, xfs, qs, ks, vs, lwh, acc,
    state, a_recv, b0_send, b1_send, yr, xt, buckets, obuf, own_f, plane_f,
    par_sem, in_sem, tail_sem, out_sem, halo_sem, a_ss, a_rs, y_ss, y_rs, x_ss, x_rs, b_ss, b_rs,
):
    me = lax.axis_index("seq")
    core = lax.axis_index("batch")
    x, y, z = me // 64, lax.rem(me // 8, 8), lax.rem(me, 8)

    def dev(xx, yy, zz):
        return (xx * 64 + yy * 8 + zz, core)

    ins = (q_hbm, k_hbm, v_hbm)

    def head_of(step):
        return lax.rem(z + 1 + step, NZ)

    def load(stream, head):
        cols = pl.ds(pl.multiple_of(head * DK, DK), DK)
        return pltpu.make_async_copy(ins[stream].at[:, cols], xin.at[stream, head], in_sem.at[stream, head])

    def tail(stream):
        return pltpu.make_async_copy(ins[stream].at[pl.ds(T - 16, 16), :], tails.at[stream], tail_sem.at[stream])

    for stream in range(3):
        tail(stream).start()
    pars = [
        pltpu.make_async_copy(src, dst, par_sem.at[i])
        for i, (src, dst) in enumerate(((cw_hbm, cw_ref), (lw_hbm, lw_ref), (gain_hbm, gain_ref)))
    ]
    for copy in pars:
        copy.start()

    def start_loads(step, carry):
        for stream in (1, 2):
            load(stream, head_of(step)).start()
        return carry

    lax.fori_loop(0, H, start_loads, 0)

    def start_q(head, carry):
        load(0, head).start()
        return carry

    lax.fori_loop(0, H, start_q, 0)

    barrier = pltpu.get_barrier_semaphore()

    def greet_ring(step, carry):
        pl.semaphore_signal(barrier, inc=1, device_id=dev(x, y, lax.rem(z + step, NZ)), device_id_type=MESH)
        pl.semaphore_signal(barrier, inc=1, device_id=dev(x, lax.rem(y + step, NY), z), device_id_type=MESH)
        return carry

    lax.fori_loop(1, NZ, greet_ring, 0)
    for step in range(1, NX):
        pl.semaphore_signal(barrier, inc=1, device_id=dev(lax.rem(x + step, NX), y, z), device_id_type=MESH)
    pl.semaphore_signal(barrier, inc=1, device_id=(lax.rem(me + 255, 256), core), device_id_type=MESH)

    halo_f[...] = jnp.zeros_like(halo_f)
    for stream in range(3):
        tail(stream).wait()
        halo_f[pl.ds(3 * stream, 3), :] = tails[stream].astype(F32)[13:16, :]
    halo_send[...] = halo_f[...].astype(BF16)
    halo = pltpu.make_async_remote_copy(
        halo_send, halo_recv, halo_sem.at[0], halo_sem.at[1], device_id=(lax.rem(me + 1, 256), core), device_id_type=MESH
    )


    ones = jnp.ones((DK, DK), BF16)

    def taps(stream, head):
        cols = pl.ds(pl.multiple_of(head * DK, DK), DK)
        return [cw_ref[stream, pl.ds(j, 1), cols] for j in range(4)]

    def silu(c):
        return c * pl.reciprocal(1.0 + jnp.exp(-c), approx=True)

    def unit(a):
        total = jnp.dot((a * a).astype(BF16), ones, preferred_element_type=F32)
        return a * lax.rsqrt(total + EPS)

    def conv_rows(src, w, row, count):
        c = w[0] * src[pl.ds(row + 5, count), :]
        for j in range(1, 4):
            c = c + w[j] * src[pl.ds(row + 5 + j, count), :]
        return silu(c)

    CH = 128

    def stream_head(stream, head, dst, halo_rows):
        w = taps(stream, head)
        buf = xf.at[stream]
        if halo_rows is None:
            buf[pl.ds(0, 8), :] = jnp.zeros((8, DK), F32)
        else:
            buf[pl.ds(5, 3), :] = halo_rows
        buf[pl.ds(8, T), :] = xin[stream, head].astype(F32)
        for row in range(0, T, CH):
            a = conv_rows(buf, w, row, CH)
            if stream < 2:
                a = unit(a)
            dst[head, pl.ds(row, CH), :] = a.astype(BF16)

    def kv_step(step, carry):
        head = head_of(step)
        for stream, dst in ((1, ks), (2, vs)):
            load(stream, head).wait()
            stream_head(stream, head, dst, None)
        return carry

    for copy in pars:
        copy.wait()
    ahead = jnp.where(z < 4, H, 2)
    lax.fori_loop(0, ahead, kv_step, 0)
    pl.semaphore_wait(barrier, 18)
    halo.start()
    lax.fori_loop(ahead, H, kv_step, 0)

    halo.wait()
    halo_f[...] = jnp.where(me == 0, 0.0, halo_recv[...].astype(F32))

    def halo_rows(stream, head):
        cols = pl.ds(pl.multiple_of(head * DK, DK), DK)
        return halo_f[pl.ds(3 * stream, 3), cols]

    def to_owner(head):
        return pltpu.make_async_remote_copy(
            state.at[head], a_recv.at[z], a_ss.at[head], a_rs.at[z], device_id=dev(x, y, head), device_id_type=MESH
        )

    def from_row(source):
        return pltpu.make_async_remote_copy(
            state.at[source], a_recv.at[source], a_ss.at[source], a_rs.at[source],
            device_id=dev(x, y, source), device_id_type=MESH,
        )

    def state_of(head):
        for stream, dst in ((1, ks), (2, vs)):
            xfs[pl.ds(5, 3), :] = halo_rows(stream, head)
            xfs[pl.ds(8, 16), :] = xin[stream, head, pl.ds(0, 16), :].astype(F32)
            a = conv_rows(xfs, taps(stream, head), 0, 16)
            if stream == 1:
                a = unit(a)
            dst[head, pl.ds(0, 16), :] = a.astype(BF16)
        return lax.dot_general(ks[head], vs[head], (((0,), (0,)), ((), ())), preferred_element_type=F32)

    def state_step(step, carry):
        head = head_of(step)
        state[head] = state_of(head).astype(BF16)
        to_owner(head).start()
        return carry

    lax.fori_loop(0, H - 1, state_step, 0)
    a_recv[z] = state_of(z).astype(BF16)

    lw = jnp.concatenate([lw_ref[...], jnp.zeros((128 - 5 * H, T), F32)], axis=0).T
    pos = lax.broadcasted_iota(jnp.int32, (T, 128), 0).astype(F32)
    lane = lax.broadcasted_iota(jnp.int32, (T, 128), 1)
    lw = jnp.where(lane < H, lw * lax.rsqrt(pos + 1.0), lw)
    for head in range(H):
        lwh[head] = lw if head == 0 else pltpu.roll(lw, 128 - head, 1)

    row_i = lax.broadcasted_iota(jnp.int32, (256, 256), 0)
    col_i = lax.broadcasted_iota(jnp.int32, (256, 256), 1)
    causal = row_i >= col_i
    NT = (((1,), (1,)), ((), ()))

    def weight(head, level):
        return jnp.broadcast_to(lwh[head, :, pl.ds(8 * level, 1)], (T, DK))

    def local_step(head, carry):
        load(0, head).wait()
        stream_head(0, head, qs, halo_rows(0, head))
        q0, q1 = qs[head, pl.ds(0, 256), :], qs[head, pl.ds(256, 256), :]
        k0, k1 = ks[head, pl.ds(0, 256), :], ks[head, pl.ds(256, 256), :]
        v0, v1 = vs[head, pl.ds(0, 256), :], vs[head, pl.ds(256, 256), :]
        s00 = jnp.where(causal, lax.dot_general(q0, k0, NT, preferred_element_type=F32), 0.0).astype(BF16)
        s10 = lax.dot_general(q1, k0, NT, preferred_element_type=F32).astype(BF16)
        s11 = jnp.where(causal, lax.dot_general(q1, k1, NT, preferred_element_type=F32), 0.0).astype(BF16)
        o0 = jnp.dot(s00, v0, preferred_element_type=F32)
        o1 = jnp.dot(s10, v0, preferred_element_type=F32) + jnp.dot(s11, v1, preferred_element_type=F32)
        w = weight(head, 0)
        acc[head, pl.ds(0, 256), :] = w[:256] * o0
        acc[head, pl.ds(256, 256), :] = w[256:] * o1
        return carry

    def from_group(first):
        def wait(source, carry):
            @pl.when(source != z)
            def _():
                from_row(source).wait_recv()

            return carry

        lax.fori_loop(first, first + 4, wait, 0)

    def group_sum(first):
        group = a_recv[first].astype(F32)
        for digit in range(1, 4):
            b0_send[first + digit] = (group * ((1.0 / (T * digit)) ** 0.5)).astype(BF16)
            group = group + a_recv[first + digit].astype(F32)
        return group

    odd = lax.rem(y, 2)
    pair = y // 2

    def needs(level, zz):
        return (lax.rem(zz, 4) != 0, (zz >= 4) | (odd == 1), pair > 0, x > 0)[level]

    def bucket_copy(level, src, to, head):
        return pltpu.make_async_remote_copy(
            src, buckets.at[level, head], b_ss.at[level, to], b_rs.at[level, head], device_id=dev(x, y, to), device_id_type=MESH
        )

    def sent(level, to):
        if level == 0:
            return b0_send.at[to]
        return b1_send.at[to // 4 if level == 1 else level]

    def send_bucket(level, first):
        def step(to, carry):
            @pl.when((to != z) & needs(level, to))
            def _():
                bucket_copy(level, sent(level, to), to, z).start()

            return carry

        lax.fori_loop(first, first + 4, step, 0)

    def row_copy(src_y, dst_y):
        return pltpu.make_async_remote_copy(
            yr.at[src_y], yr.at[src_y], y_ss.at[dst_y], y_rs.at[src_y], device_id=dev(x, dst_y, z), device_id_type=MESH
        )

    def plane_copy(src_x, dst_x):
        return pltpu.make_async_remote_copy(
            xt.at[src_x], xt.at[src_x], x_ss.at[dst_x], x_rs.at[src_x], device_id=dev(dst_x, y, z), device_id_type=MESH
        )

    lax.fori_loop(0, 4, local_step, 0)
    from_group(0)
    own_f[0] = group_sum(0)
    send_bucket(0, 0)
    lax.fori_loop(4, H, local_step, 0)

    from_group(4)
    yr[y] = (own_f[0] + group_sum(4)).astype(BF16)

    def send_rows(step, carry):
        row_copy(y, lax.rem(y + step, NY)).start()
        return carry

    lax.fori_loop(1, NY, send_rows, 0)

    @pl.when(needs(0, z))
    def _():
        buckets[0, z] = b0_send[z]


    def wait_rows(step, carry):
        src = lax.rem(y + NY - step, NY)
        row_copy(src, src).wait_recv()
        return carry

    wait_rows(1, 0)
    before = jnp.where(odd == 1, 1.0, 0.0) * yr[jnp.maximum(y - 1, 0)].astype(F32)
    b1_send[0] = (level_factor(2 * odd, 1) * before).astype(BF16)
    b1_send[1] = (level_factor(2 * odd + 1, 1) * (before + own_f[0])).astype(BF16)
    send_bucket(1, 0)
    send_bucket(0, 4)
    buckets[1, z] = b1_send[z // 4]

    lax.fori_loop(2, NY, wait_rows, 0)
    earlier = jnp.zeros((DK, DK), F32)
    plane = jnp.zeros((DK, DK), F32)
    for yy in range(NY):
        r = yr[yy].astype(F32)
        plane = plane + r
        earlier = earlier + jnp.where(yy < 2 * pair, 1.0, 0.0) * r
    xt[x] = plane.astype(BF16)
    for xx in range(1, NX):

        @pl.when(xx > x)
        def _():
            plane_copy(x, xx).start()

    b1_send[2] = (level_factor(pair, 2) * earlier).astype(BF16)
    send_bucket(2, 0)
    send_bucket(1, 4)
    buckets[2, z] = b1_send[2]

    plane_f[...] = jnp.zeros((DK, DK), F32)
    for xx in range(NX - 1):

        @pl.when(xx < x)
        def _():
            plane_copy(xx, xx).wait_recv()
            plane_f[...] += xt[xx].astype(F32)

    b1_send[3] = (level_factor(x, 3) * plane_f[...]).astype(BF16)
    send_bucket(3, 0)
    send_bucket(2, 4)
    send_bucket(3, 4)
    buckets[3, z] = b1_send[3]

    def wait_bucket(level, head):
        @pl.when(head != z)
        def _():
            bucket_copy(level, b1_send.at[3], head, head).wait_recv()

    def project(level, head):
        return weight(head, level + 1) * jnp.dot(qs[head], buckets[level, head], preferred_element_type=F32)

    def add_level(level):
        def step(i, carry):
            head = lax.rem(z + i, NZ)
            wait_bucket(level, head)
            acc[head] += project(level, head)
            return carry

        @pl.when(needs(level, z))
        def _():
            lax.fori_loop(0, H, step, 0)

    add_level(0)
    add_level(1)
    add_level(2)

    def store(head):
        cols = pl.ds(pl.multiple_of(head * DK, DK), DK)
        return pltpu.make_async_copy(obuf.at[head], out_hbm.at[:, cols], out_sem.at[head])

    def last_step(i, carry):
        head = lax.rem(z + i, NZ)

        @pl.when(x > 0)
        def _():
            wait_bucket(3, head)

        mixed = acc[head] + project(3, head)
        total = jnp.dot((mixed * mixed).astype(BF16), ones, preferred_element_type=F32)
        cols = pl.ds(pl.multiple_of(head * DK, DK), DK)
        obuf[head] = (mixed * lax.rsqrt(total * (1.0 / DK) + EPS) * gain_ref[:, cols]).astype(BF16)
        store(head).start()
        return carry

    @pl.when(x == 0)
    def _():
        for head in range(H):
            buckets[3, head] = jnp.zeros((DK, DK), BF16)

    lax.fori_loop(0, H, last_step, 0)

    def drain(step, carry):
        to = lax.rem(z + step, NZ)
        from_row(to).wait_send()
        row_copy(y, lax.rem(y + step, NY)).wait_send()
        for level in range(4):

            @pl.when(needs(level, to))
            def _():
                bucket_copy(level, b1_send.at[3], to, z).wait_send()

        return carry

    lax.fori_loop(1, NZ, drain, 0)
    for xx in range(1, NX):

        @pl.when(xx > x)
        def _():
            plane_copy(x, xx).wait_send()

    def stored(head, carry):
        store(head).wait()
        return carry

    lax.fori_loop(0, H, stored, 0)


def shards(query_in, key_in, value_in, conv_weight, level_weights, out_gain):
    hbm = pl.BlockSpec(memory_space=pltpu.HBM)
    dma = pltpu.SemaphoreType.DMA
    return pl.pallas_call(
        kernel,
        out_shape=jax.ShapeDtypeStruct((T, H * DK), BF16),
        in_specs=[hbm] * 6,
        out_specs=hbm,
        scratch_shapes=[
            pltpu.VMEM((3, 4, H * DK), F32),
            pltpu.VMEM((5 * H, T), F32),
            pltpu.VMEM((1, H * DK), F32),
            pltpu.VMEM((3, H, T, DK), BF16),
            pltpu.VMEM((3, 16, H * DK), BF16),
            pltpu.VMEM((16, H * DK), F32),
            pltpu.VMEM((16, H * DK), BF16),
            pltpu.VMEM((16, H * DK), BF16),
            pltpu.VMEM((3, T + 8, DK), F32),
            pltpu.VMEM((24, DK), F32),
            pltpu.VMEM((H, T, DK), BF16),
            pltpu.VMEM((H, T, DK), BF16),
            pltpu.VMEM((H, T, DK), BF16),
            pltpu.VMEM((H, T, DK), F32),
            pltpu.VMEM((H, T, DK), F32),
            pltpu.VMEM((H, DK, DK), BF16),
            pltpu.VMEM((NZ, DK, DK), BF16),
            pltpu.VMEM((NZ, DK, DK), BF16),
            pltpu.VMEM((4, DK, DK), BF16),
            pltpu.VMEM((NY, DK, DK), BF16),
            pltpu.VMEM((NX, DK, DK), BF16),
            pltpu.VMEM((4, H, DK, DK), BF16),
            pltpu.VMEM((H, T, DK), BF16),
            pltpu.VMEM((1, DK, DK), F32),
            pltpu.VMEM((DK, DK), F32),
            dma((3,)),
            dma((3, H)),
            dma((3,)),
            dma((H,)),
            dma((2,)),
            dma((NZ,)),
            dma((NZ,)),
            dma((NY,)),
            dma((NY,)),
            dma((NX,)),
            dma((NX,)),
            dma((4, NZ)),
            dma((4, NZ)),
        ],
        compiler_params=pltpu.CompilerParams(
            collective_id=0, has_side_effects=True, vmem_limit_bytes=60 * 1024 * 1024
        ),
        cost_estimate=pl.CostEstimate(flops=2 * 10**9, bytes_accessed=4 * 2**20, transcendentals=2 * 10**6),
    )(query_in, key_in, value_in, conv_weight, level_weights.reshape(5 * H, T), out_gain.reshape(1, H * DK))


def solution(mesh):
    return jax.shard_map(
        shards,
        mesh=mesh,
        in_specs=(
            P(("batch", "seq"), None),
            P(("batch", "seq"), None),
            P(("batch", "seq"), None),
            P(),
            P(None, None, ("batch", "seq")),
            P(),
        ),
        out_specs=P(("batch", "seq"), None),
        check_vma=False,
    )
```

```python
import functools

import jax
import jax.numpy as jnp
from jax import lax
from jax.experimental import pallas as pl
from jax.experimental.pallas import tpu as pltpu
from jax.sharding import PartitionSpec as P

MESH = pl.DeviceIdType.MESH
EPS = 1e-6
H = 8
DK = 128
T = 512
NX, NY, NZ = 4, 8, 8
F32 = jnp.float32
BF16 = jnp.bfloat16


def level_factor(digit, level):
    base = (1.0 / (T * 4.0**level)) ** 0.5
    return jnp.where(
        digit == 0, 0.0, jnp.where(digit == 1, base, jnp.where(digit == 2, base * 0.5**0.5, base * (1.0 / 3.0) ** 0.5))
    )


def kernel(
    q_hbm, k_hbm, v_hbm, cw_hbm, lw_hbm, gain_hbm, out_hbm,
    cw_ref, lw_ref, gain_ref,
    xin, tails, halo_f, halo_send, halo_recv, xf, xfs, qs, ks, vs, lwh, acc,
    state, a_recv, b0_send, b1_send, yr, xt, buckets, obuf, own_f, plane_f,
    par_sem, in_sem, tail_sem, out_sem, halo_sem, a_ss, a_rs, y_ss, y_rs, x_ss, x_rs, b_ss, b_rs,
):
    me = lax.axis_index("seq")
    core = lax.axis_index("batch")
    x, y, z = me // 64, lax.rem(me // 8, 8), lax.rem(me, 8)

    def dev(xx, yy, zz):
        return (xx * 64 + yy * 8 + zz, core)

    ins = (q_hbm, k_hbm, v_hbm)

    def head_of(step):
        return lax.rem(z + 1 + step, NZ)

    def load(stream, head):
        cols = pl.ds(pl.multiple_of(head * DK, DK), DK)
        return pltpu.make_async_copy(ins[stream].at[:, cols], xin.at[stream, head], in_sem.at[stream, head])

    def tail(stream):
        return pltpu.make_async_copy(ins[stream].at[pl.ds(T - 16, 16), :], tails.at[stream], tail_sem.at[stream])

    for stream in range(3):
        tail(stream).start()
    pars = [
        pltpu.make_async_copy(src, dst, par_sem.at[i])
        for i, (src, dst) in enumerate(((cw_hbm, cw_ref), (lw_hbm, lw_ref), (gain_hbm, gain_ref)))
    ]
    for copy in pars:
        copy.start()

    def start_loads(step, carry):
        for stream in (1, 2):
            load(stream, head_of(step)).start()
        return carry

    lax.fori_loop(0, H, start_loads, 0)

    def start_q(head, carry):
        load(0, head).start()
        return carry

    lax.fori_loop(0, H, start_q, 0)

    barrier = pltpu.get_barrier_semaphore()

    def greet_ring(step, carry):
        pl.semaphore_signal(barrier, inc=1, device_id=dev(x, y, lax.rem(z + step, NZ)), device_id_type=MESH)
        pl.semaphore_signal(barrier, inc=1, device_id=dev(x, lax.rem(y + step, NY), z), device_id_type=MESH)
        return carry

    lax.fori_loop(1, NZ, greet_ring, 0)
    for step in range(1, NX):
        pl.semaphore_signal(barrier, inc=1, device_id=dev(lax.rem(x + step, NX), y, z), device_id_type=MESH)
    pl.semaphore_signal(barrier, inc=1, device_id=(lax.rem(me + 255, 256), core), device_id_type=MESH)

    halo_f[...] = jnp.zeros_like(halo_f)
    for stream in range(3):
        tail(stream).wait()
        halo_f[pl.ds(3 * stream, 3), :] = tails[stream].astype(F32)[13:16, :]
    halo_send[...] = halo_f[...].astype(BF16)
    halo = pltpu.make_async_remote_copy(
        halo_send, halo_recv, halo_sem.at[0], halo_sem.at[1], device_id=(lax.rem(me + 1, 256), core), device_id_type=MESH
    )


    def taps(stream, head):
        cols = pl.ds(pl.multiple_of(head * DK, DK), DK)
        return [cw_ref[stream, pl.ds(j, 1), cols] for j in range(4)]

    def silu(c):
        return c * pl.reciprocal(1.0 + jnp.exp(-c), approx=True)

    def unit(a):
        return a * lax.rsqrt(jnp.sum(a * a, axis=-1, keepdims=True) + EPS)

    def conv_rows(src, w, row, count):
        c = w[0] * src[pl.ds(row + 5, count), :]
        for j in range(1, 4):
            c = c + w[j] * src[pl.ds(row + 5 + j, count), :]
        return silu(c)

    CH = 128

    def stream_head(stream, head, dst, halo_rows):
        w = taps(stream, head)
        buf = xf.at[stream]
        if halo_rows is None:
            buf[pl.ds(0, 8), :] = jnp.zeros((8, DK), F32)
        else:
            buf[pl.ds(5, 3), :] = halo_rows
        buf[pl.ds(8, T), :] = xin[stream, head].astype(F32)
        for row in range(0, T, CH):
            a = conv_rows(buf, w, row, CH)
            if stream < 2:
                a = unit(a)
            dst[head, pl.ds(row, CH), :] = a.astype(BF16)

    def kv_step(step, carry):
        head = head_of(step)
        for stream, dst in ((1, ks), (2, vs)):
            load(stream, head).wait()
            stream_head(stream, head, dst, None)
        return carry

    for copy in pars:
        copy.wait()
    ahead = jnp.where(z < 4, H, 2)
    lax.fori_loop(0, ahead, kv_step, 0)
    pl.semaphore_wait(barrier, 18)
    halo.start()
    lax.fori_loop(ahead, H, kv_step, 0)

    halo.wait()
    halo_f[...] = jnp.where(me == 0, 0.0, halo_recv[...].astype(F32))

    def halo_rows(stream, head):
        cols = pl.ds(pl.multiple_of(head * DK, DK), DK)
        return halo_f[pl.ds(3 * stream, 3), cols]

    def to_owner(head):
        return pltpu.make_async_remote_copy(
            state.at[head], a_recv.at[z], a_ss.at[head], a_rs.at[z], device_id=dev(x, y, head), device_id_type=MESH
        )

    def from_row(source):
        return pltpu.make_async_remote_copy(
            state.at[source], a_recv.at[source], a_ss.at[source], a_rs.at[source],
            device_id=dev(x, y, source), device_id_type=MESH,
        )

    for stream, dst in ((1, ks), (2, vs)):
        for head in range(H):
            cols = slice(head * DK, (head + 1) * DK)
            xfs[stream - 1, head, pl.ds(5, 3), :] = halo_f[3 * stream : 3 * stream + 3, cols]
            xfs[stream - 1, head, pl.ds(8, 16), :] = xin[stream, head, pl.ds(0, 16), :].astype(F32)
    for stream, dst in ((1, ks), (2, vs)):
        for head in range(H):
            a = conv_rows(xfs.at[stream - 1, head], taps(stream, head), 0, 16)
            if stream == 1:
                a = unit(a)
            dst[head, pl.ds(0, 16), :] = a.astype(BF16)

    def state_of(head):
        return lax.dot_general(ks[head], vs[head], (((0,), (0,)), ((), ())), preferred_element_type=F32)

    def state_step(step, carry):
        head = head_of(step)
        state[head] = state_of(head).astype(BF16)
        to_owner(head).start()
        return carry

    lax.fori_loop(0, H - 1, state_step, 0)
    a_recv[z] = state_of(z).astype(BF16)

    lw = jnp.concatenate([lw_ref[...], jnp.zeros((128 - 5 * H, T), F32)], axis=0).T
    pos = lax.broadcasted_iota(jnp.int32, (T, 128), 0).astype(F32)
    lane = lax.broadcasted_iota(jnp.int32, (T, 128), 1)
    lw = jnp.where(lane < H, lw * lax.rsqrt(pos + 1.0), lw)
    for head in range(H):
        lwh[head] = lw if head == 0 else pltpu.roll(lw, 128 - head, 1)

    row_i = lax.broadcasted_iota(jnp.int32, (256, 256), 0)
    col_i = lax.broadcasted_iota(jnp.int32, (256, 256), 1)
    causal = row_i >= col_i
    NT = (((1,), (1,)), ((), ()))

    def weight(head, level):
        return jnp.broadcast_to(lwh[head, :, pl.ds(8 * level, 1)], (T, DK))

    def local_step(head, carry):
        load(0, head).wait()
        stream_head(0, head, qs, halo_rows(0, head))
        q0, q1 = qs[head, pl.ds(0, 256), :], qs[head, pl.ds(256, 256), :]
        k0, k1 = ks[head, pl.ds(0, 256), :], ks[head, pl.ds(256, 256), :]
        v0, v1 = vs[head, pl.ds(0, 256), :], vs[head, pl.ds(256, 256), :]
        s00 = jnp.where(causal, lax.dot_general(q0, k0, NT, preferred_element_type=F32), 0.0).astype(BF16)
        s10 = lax.dot_general(q1, k0, NT, preferred_element_type=F32).astype(BF16)
        s11 = jnp.where(causal, lax.dot_general(q1, k1, NT, preferred_element_type=F32), 0.0).astype(BF16)
        o0 = jnp.dot(s00, v0, preferred_element_type=F32)
        o1 = jnp.dot(s10, v0, preferred_element_type=F32) + jnp.dot(s11, v1, preferred_element_type=F32)
        w = weight(head, 0)
        acc[head, pl.ds(0, 256), :] = w[:256] * o0
        acc[head, pl.ds(256, 256), :] = w[256:] * o1
        return carry

    def from_group(first):
        def wait(source, carry):
            @pl.when(source != z)
            def _():
                from_row(source).wait_recv()

            return carry

        lax.fori_loop(first, first + 4, wait, 0)

    def group_sum(first):
        group = a_recv[first].astype(F32)
        for digit in range(1, 4):
            b0_send[first + digit] = (group * ((1.0 / (T * digit)) ** 0.5)).astype(BF16)
            group = group + a_recv[first + digit].astype(F32)
        return group

    odd = lax.rem(y, 2)
    pair = y // 2

    def needs(level, zz):
        return (lax.rem(zz, 4) != 0, (zz >= 4) | (odd == 1), pair > 0, x > 0)[level]

    def bucket_copy(level, src, to, head):
        return pltpu.make_async_remote_copy(
            src, buckets.at[level, head], b_ss.at[level, to], b_rs.at[level, head], device_id=dev(x, y, to), device_id_type=MESH
        )

    def sent(level, to):
        if level == 0:
            return b0_send.at[to]
        return b1_send.at[to // 4 if level == 1 else level]

    def send_bucket(level, first):
        def step(to, carry):
            @pl.when((to != z) & needs(level, to))
            def _():
                bucket_copy(level, sent(level, to), to, z).start()

            return carry

        lax.fori_loop(first, first + 4, step, 0)

    def row_copy(src_y, dst_y):
        return pltpu.make_async_remote_copy(
            yr.at[src_y], yr.at[src_y], y_ss.at[dst_y], y_rs.at[src_y], device_id=dev(x, dst_y, z), device_id_type=MESH
        )

    def plane_copy(src_x, dst_x):
        return pltpu.make_async_remote_copy(
            xt.at[src_x], xt.at[src_x], x_ss.at[dst_x], x_rs.at[src_x], device_id=dev(dst_x, y, z), device_id_type=MESH
        )

    lax.fori_loop(0, 3, local_step, 0)
    from_group(0)
    own_f[0] = group_sum(0)
    send_bucket(0, 0)
    lax.fori_loop(3, 6, local_step, 0)

    from_group(4)
    yr[y] = (own_f[0] + group_sum(4)).astype(BF16)

    def send_rows(step, carry):
        row_copy(y, lax.rem(y + step, NY)).start()
        return carry

    lax.fori_loop(1, NY, send_rows, 0)

    @pl.when(needs(0, z))
    def _():
        buckets[0, z] = b0_send[z]


    def wait_rows(step, carry):
        src = lax.rem(y + NY - step, NY)
        row_copy(src, src).wait_recv()
        return carry

    lax.fori_loop(6, H, local_step, 0)
    wait_rows(1, 0)
    before = jnp.where(odd == 1, 1.0, 0.0) * yr[jnp.maximum(y - 1, 0)].astype(F32)
    b1_send[0] = (level_factor(2 * odd, 1) * before).astype(BF16)
    b1_send[1] = (level_factor(2 * odd + 1, 1) * (before + own_f[0])).astype(BF16)
    send_bucket(1, 0)
    send_bucket(0, 4)
    buckets[1, z] = b1_send[z // 4]

    lax.fori_loop(2, NY, wait_rows, 0)
    earlier = jnp.zeros((DK, DK), F32)
    plane = jnp.zeros((DK, DK), F32)
    for yy in range(NY):
        r = yr[yy].astype(F32)
        plane = plane + r
        earlier = earlier + jnp.where(yy < 2 * pair, 1.0, 0.0) * r
    xt[x] = plane.astype(BF16)
    for xx in range(1, NX):

        @pl.when(xx > x)
        def _():
            plane_copy(x, xx).start()

    b1_send[2] = (level_factor(pair, 2) * earlier).astype(BF16)
    send_bucket(2, 0)
    send_bucket(1, 4)
    buckets[2, z] = b1_send[2]

    plane_f[...] = jnp.zeros((DK, DK), F32)
    for xx in range(NX - 1):

        @pl.when(xx < x)
        def _():
            plane_copy(xx, xx).wait_recv()
            plane_f[...] += xt[xx].astype(F32)

    b1_send[3] = (level_factor(x, 3) * plane_f[...]).astype(BF16)
    send_bucket(3, 0)
    send_bucket(2, 4)
    send_bucket(3, 4)
    buckets[3, z] = b1_send[3]

    def wait_bucket(level, head):
        @pl.when(head != z)
        def _():
            bucket_copy(level, b1_send.at[3], head, head).wait_recv()

    def project(level, head):
        return weight(head, level + 1) * jnp.dot(qs[head], buckets[level, head], preferred_element_type=F32)

    def wait_level(level, first):
        def step(head, carry):
            wait_bucket(level, head)
            return carry

        @pl.when(needs(level, z))
        def _():
            lax.fori_loop(first, first + 4, step, 0)

    def add_level(level):
        @pl.when(needs(level, z))
        def _():
            for first in (0, 4):
                wait_level(level, first)
                for head in range(first, first + 4):
                    acc[head] += project(level, head)

    def store(head):
        cols = pl.ds(head * DK, DK)
        return pltpu.make_async_copy(obuf.at[head], out_hbm.at[:, cols], out_sem.at[head])

    def clear(level):
        @pl.when(jnp.logical_not(needs(level, z)))
        def _():
            for head in range(H):
                buckets[level, head] = jnp.zeros((DK, DK), BF16)

    clear(2)
    clear(3)
    add_level(0)
    add_level(1)
    for first in (0, 4):
        wait_level(2, first)
        wait_level(3, first)
        for head in range(first, first + 4):
            mixed = acc[head] + project(2, head) + project(3, head)
            mean = jnp.sum(mixed * mixed, axis=-1, keepdims=True) * (1.0 / DK)
            gain = gain_ref[:, head * DK : (head + 1) * DK]
            obuf[head] = (mixed * lax.rsqrt(mean + EPS) * gain).astype(BF16)
            store(head).start()

    def drain(step, carry):
        to = lax.rem(z + step, NZ)
        from_row(to).wait_send()
        row_copy(y, lax.rem(y + step, NY)).wait_send()
        for level in range(4):

            @pl.when(needs(level, to))
            def _():
                bucket_copy(level, b1_send.at[3], to, z).wait_send()

        return carry

    lax.fori_loop(1, NZ, drain, 0)
    for xx in range(1, NX):

        @pl.when(xx > x)
        def _():
            plane_copy(x, xx).wait_send()

    for head in range(H):
        store(head).wait()


def shards(query_in, key_in, value_in, conv_weight, level_weights, out_gain):
    hbm = pl.BlockSpec(memory_space=pltpu.HBM)
    dma = pltpu.SemaphoreType.DMA
    return pl.pallas_call(
        kernel,
        out_shape=jax.ShapeDtypeStruct((T, H * DK), BF16),
        in_specs=[hbm] * 6,
        out_specs=hbm,
        scratch_shapes=[
            pltpu.VMEM((3, 4, H * DK), F32),
            pltpu.VMEM((5 * H, T), F32),
            pltpu.VMEM((1, H * DK), F32),
            pltpu.VMEM((3, H, T, DK), BF16),
            pltpu.VMEM((3, 16, H * DK), BF16),
            pltpu.VMEM((16, H * DK), F32),
            pltpu.VMEM((16, H * DK), BF16),
            pltpu.VMEM((16, H * DK), BF16),
            pltpu.VMEM((3, T + 8, DK), F32),
            pltpu.VMEM((2, H, 24, DK), F32),
            pltpu.VMEM((H, T, DK), BF16),
            pltpu.VMEM((H, T, DK), BF16),
            pltpu.VMEM((H, T, DK), BF16),
            pltpu.VMEM((H, T, DK), F32),
            pltpu.VMEM((H, T, DK), F32),
            pltpu.VMEM((H, DK, DK), BF16),
            pltpu.VMEM((NZ, DK, DK), BF16),
            pltpu.VMEM((NZ, DK, DK), BF16),
            pltpu.VMEM((4, DK, DK), BF16),
            pltpu.VMEM((NY, DK, DK), BF16),
            pltpu.VMEM((NX, DK, DK), BF16),
            pltpu.VMEM((4, H, DK, DK), BF16),
            pltpu.VMEM((H, T, DK), BF16),
            pltpu.VMEM((1, DK, DK), F32),
            pltpu.VMEM((DK, DK), F32),
            dma((3,)),
            dma((3, H)),
            dma((3,)),
            dma((H,)),
            dma((2,)),
            dma((NZ,)),
            dma((NZ,)),
            dma((NY,)),
            dma((NY,)),
            dma((NX,)),
            dma((NX,)),
            dma((4, NZ)),
            dma((4, NZ)),
        ],
        compiler_params=pltpu.CompilerParams(
            collective_id=0, has_side_effects=True, vmem_limit_bytes=60 * 1024 * 1024
        ),
        cost_estimate=pl.CostEstimate(flops=2 * 10**9, bytes_accessed=4 * 2**20, transcendentals=2 * 10**6),
    )(query_in, key_in, value_in, conv_weight, level_weights.reshape(5 * H, T), out_gain.reshape(1, H * DK))


def solution(mesh):
    return jax.shard_map(
        shards,
        mesh=mesh,
        in_specs=(
            P(("batch", "seq"), None),
            P(("batch", "seq"), None),
            P(("batch", "seq"), None),
            P(),
            P(None, None, ("batch", "seq")),
            P(),
        ),
        out_specs=P(("batch", "seq"), None),
        check_vma=False,
    )
```

```python
import functools

import jax
import jax.numpy as jnp
from jax import lax
from jax.experimental import pallas as pl
from jax.experimental.pallas import tpu as pltpu
from jax.sharding import PartitionSpec as P

MESH = pl.DeviceIdType.MESH
EPS = 1e-6
H = 8
DK = 128
T = 512
NX, NY, NZ = 4, 8, 8
F32 = jnp.float32
BF16 = jnp.bfloat16


def level_factor(digit, level):
    base = (1.0 / (T * 4.0**level)) ** 0.5
    return jnp.where(
        digit == 0, 0.0, jnp.where(digit == 1, base, jnp.where(digit == 2, base * 0.5**0.5, base * (1.0 / 3.0) ** 0.5))
    )


def kernel(
    q_hbm, k_hbm, v_hbm, cw_hbm, lw_hbm, gain_hbm, out_hbm,
    cw_ref, lw_ref, gain_ref,
    xin, tails, halo_f, halo_send, halo_recv, xf, xfs, qs, ks, vs, lwh, acc,
    state, a_recv, b0_send, b1_send, yr, xt, buckets, obuf, own_f, plane_f,
    par_sem, in_sem, tail_sem, out_sem, halo_sem, a_ss, a_rs, y_ss, y_rs, x_ss, x_rs, b_ss, b_rs,
):
    me = lax.axis_index("seq")
    core = lax.axis_index("batch")
    x, y, z = me // 64, lax.rem(me // 8, 8), lax.rem(me, 8)

    def dev(xx, yy, zz):
        return (xx * 64 + yy * 8 + zz, core)

    ins = (q_hbm, k_hbm, v_hbm)

    def head_of(step):
        return lax.rem(z + 1 + step, NZ)

    def load(stream, head):
        cols = pl.ds(pl.multiple_of(head * DK, DK), DK)
        return pltpu.make_async_copy(ins[stream].at[:, cols], xin.at[stream, head], in_sem.at[stream, head])

    def tail(stream):
        return pltpu.make_async_copy(ins[stream].at[pl.ds(T - 16, 16), :], tails.at[stream], tail_sem.at[stream])

    for stream in range(3):
        tail(stream).start()
    pars = [
        pltpu.make_async_copy(src, dst, par_sem.at[i])
        for i, (src, dst) in enumerate(((cw_hbm, cw_ref), (lw_hbm, lw_ref), (gain_hbm, gain_ref)))
    ]
    for copy in pars:
        copy.start()

    def start_loads(step, carry):
        for stream in (1, 2):
            load(stream, head_of(step)).start()
        return carry

    lax.fori_loop(0, H, start_loads, 0)

    def start_q(head, carry):
        load(0, head).start()
        return carry

    lax.fori_loop(0, H, start_q, 0)

    barrier = pltpu.get_barrier_semaphore()

    def greet_ring(step, carry):
        pl.semaphore_signal(barrier, inc=1, device_id=dev(x, y, lax.rem(z + step, NZ)), device_id_type=MESH)
        pl.semaphore_signal(barrier, inc=1, device_id=dev(x, lax.rem(y + step, NY), z), device_id_type=MESH)
        return carry

    lax.fori_loop(1, NZ, greet_ring, 0)
    for step in range(1, NX):
        pl.semaphore_signal(barrier, inc=1, device_id=dev(lax.rem(x + step, NX), y, z), device_id_type=MESH)
    pl.semaphore_signal(barrier, inc=1, device_id=(lax.rem(me + 255, 256), core), device_id_type=MESH)

    halo_f[...] = jnp.zeros_like(halo_f)
    for stream in range(3):
        tail(stream).wait()
        halo_f[pl.ds(3 * stream, 3), :] = tails[stream].astype(F32)[13:16, :]
    halo_send[...] = halo_f[...].astype(BF16)
    halo = pltpu.make_async_remote_copy(
        halo_send, halo_recv, halo_sem.at[0], halo_sem.at[1], device_id=(lax.rem(me + 1, 256), core), device_id_type=MESH
    )


    def taps(stream, head):
        cols = pl.ds(pl.multiple_of(head * DK, DK), DK)
        return [cw_ref[stream, pl.ds(j, 1), cols] for j in range(4)]

    def silu(c):
        return c * pl.reciprocal(1.0 + jnp.exp(-c), approx=True)

    def unit(a):
        return a * lax.rsqrt(jnp.sum(a * a, axis=-1, keepdims=True) + EPS)

    def conv_rows(src, w, row, count):
        c = w[0] * src[pl.ds(row + 5, count), :]
        for j in range(1, 4):
            c = c + w[j] * src[pl.ds(row + 5 + j, count), :]
        return silu(c)

    CH = 128

    def stream_head(stream, head, dst, halo_rows):
        w = taps(stream, head)
        buf = xf.at[stream]
        if halo_rows is None:
            buf[pl.ds(0, 8), :] = jnp.zeros((8, DK), F32)
        else:
            buf[pl.ds(5, 3), :] = halo_rows
        buf[pl.ds(8, T), :] = xin[stream, head].astype(F32)
        for row in range(0, T, CH):
            a = conv_rows(buf, w, row, CH)
            if stream < 2:
                a = unit(a)
            dst[head, pl.ds(row, CH), :] = a.astype(BF16)

    def kv_step(step, carry):
        head = head_of(step)
        for stream, dst in ((1, ks), (2, vs)):
            load(stream, head).wait()
            stream_head(stream, head, dst, None)
        return carry

    for copy in pars:
        copy.wait()
    ahead = jnp.where(z < 4, 4, 1)
    lax.fori_loop(0, ahead, kv_step, 0)
    pl.semaphore_wait(barrier, 18)
    halo.start()
    lax.fori_loop(ahead, H, kv_step, 0)

    halo.wait()
    halo_f[...] = jnp.where(me == 0, 0.0, halo_recv[...].astype(F32))

    def halo_rows(stream, head):
        cols = pl.ds(pl.multiple_of(head * DK, DK), DK)
        return halo_f[pl.ds(3 * stream, 3), cols]

    def to_owner(head):
        return pltpu.make_async_remote_copy(
            state.at[head], a_recv.at[z], a_ss.at[head], a_rs.at[z], device_id=dev(x, y, head), device_id_type=MESH
        )

    def from_row(source):
        return pltpu.make_async_remote_copy(
            state.at[source], a_recv.at[source], a_ss.at[source], a_rs.at[source],
            device_id=dev(x, y, source), device_id_type=MESH,
        )

    for stream, dst in ((1, ks), (2, vs)):
        for head in range(H):
            cols = slice(head * DK, (head + 1) * DK)
            xfs[stream - 1, head, pl.ds(5, 3), :] = halo_f[3 * stream : 3 * stream + 3, cols]
            xfs[stream - 1, head, pl.ds(8, 16), :] = xin[stream, head, pl.ds(0, 16), :].astype(F32)
    for stream, dst in ((1, ks), (2, vs)):
        for head in range(H):
            a = conv_rows(xfs.at[stream - 1, head], taps(stream, head), 0, 16)
            if stream == 1:
                a = unit(a)
            dst[head, pl.ds(0, 16), :] = a.astype(BF16)

    def state_of(head):
        return lax.dot_general(ks[head], vs[head], (((0,), (0,)), ((), ())), preferred_element_type=F32)

    def state_step(step, carry):
        head = head_of(step)
        state[head] = state_of(head).astype(BF16)
        to_owner(head).start()
        return carry

    lax.fori_loop(0, H - 1, state_step, 0)
    a_recv[z] = state_of(z).astype(BF16)

    lw = jnp.concatenate([lw_ref[...], jnp.zeros((128 - 5 * H, T), F32)], axis=0).T
    pos = lax.broadcasted_iota(jnp.int32, (T, 128), 0).astype(F32)
    lane = lax.broadcasted_iota(jnp.int32, (T, 128), 1)
    lw = jnp.where(lane < H, lw * lax.rsqrt(pos + 1.0), lw)
    for head in range(H):
        lwh[head] = lw if head == 0 else pltpu.roll(lw, 128 - head, 1)

    row_i = lax.broadcasted_iota(jnp.int32, (256, 256), 0)
    col_i = lax.broadcasted_iota(jnp.int32, (256, 256), 1)
    causal = row_i >= col_i
    NT = (((1,), (1,)), ((), ()))

    def weight(head, level):
        return jnp.broadcast_to(lwh[head, :, pl.ds(8 * level, 1)], (T, DK))

    def local_step(head, carry):
        load(0, head).wait()
        stream_head(0, head, qs, halo_rows(0, head))
        q0, q1 = qs[head, pl.ds(0, 256), :], qs[head, pl.ds(256, 256), :]
        k0, k1 = ks[head, pl.ds(0, 256), :], ks[head, pl.ds(256, 256), :]
        v0, v1 = vs[head, pl.ds(0, 256), :], vs[head, pl.ds(256, 256), :]
        s00 = jnp.where(causal, lax.dot_general(q0, k0, NT, preferred_element_type=F32), 0.0).astype(BF16)
        s10 = lax.dot_general(q1, k0, NT, preferred_element_type=F32).astype(BF16)
        s11 = jnp.where(causal, lax.dot_general(q1, k1, NT, preferred_element_type=F32), 0.0).astype(BF16)
        o0 = jnp.dot(s00, v0, preferred_element_type=F32)
        o1 = jnp.dot(s10, v0, preferred_element_type=F32) + jnp.dot(s11, v1, preferred_element_type=F32)
        w = weight(head, 0)
        acc[head, pl.ds(0, 256), :] = w[:256] * o0
        acc[head, pl.ds(256, 256), :] = w[256:] * o1
        return carry

    def from_group(first):
        def wait(source, carry):
            @pl.when(source != z)
            def _():
                from_row(source).wait_recv()

            return carry

        lax.fori_loop(first, first + 4, wait, 0)

    def group_sum(first):
        group = a_recv[first].astype(F32)
        for digit in range(1, 4):
            b0_send[first + digit] = (group * ((1.0 / (T * digit)) ** 0.5)).astype(BF16)
            group = group + a_recv[first + digit].astype(F32)
        return group

    odd = lax.rem(y, 2)
    pair = y // 2

    def needs(level, zz):
        return (lax.rem(zz, 4) != 0, (zz >= 4) | (odd == 1), pair > 0, x > 0)[level]

    def bucket_copy(level, src, to, head):
        return pltpu.make_async_remote_copy(
            src, buckets.at[level, head], b_ss.at[level, to], b_rs.at[level, head], device_id=dev(x, y, to), device_id_type=MESH
        )

    def sent(level, to):
        if level == 0:
            return b0_send.at[to]
        return b1_send.at[to // 4 if level == 1 else level]

    def send_bucket(level, first):
        def step(to, carry):
            @pl.when((to != z) & needs(level, to))
            def _():
                bucket_copy(level, sent(level, to), to, z).start()

            return carry

        lax.fori_loop(first, first + 4, step, 0)

    def row_copy(src_y, dst_y):
        return pltpu.make_async_remote_copy(
            yr.at[src_y], yr.at[src_y], y_ss.at[dst_y], y_rs.at[src_y], device_id=dev(x, dst_y, z), device_id_type=MESH
        )

    def plane_copy(src_x, dst_x):
        return pltpu.make_async_remote_copy(
            xt.at[src_x], xt.at[src_x], x_ss.at[dst_x], x_rs.at[src_x], device_id=dev(dst_x, y, z), device_id_type=MESH
        )

    lax.fori_loop(0, 3, local_step, 0)
    from_group(0)
    own_f[0] = group_sum(0)
    send_bucket(0, 0)
    lax.fori_loop(3, 6, local_step, 0)

    from_group(4)
    yr[y] = (own_f[0] + group_sum(4)).astype(BF16)

    def send_rows(step, carry):
        row_copy(y, lax.rem(y + step, NY)).start()
        return carry

    lax.fori_loop(1, NY, send_rows, 0)

    @pl.when(needs(0, z))
    def _():
        buckets[0, z] = b0_send[z]


    def wait_rows(step, carry):
        src = lax.rem(y + NY - step, NY)
        row_copy(src, src).wait_recv()
        return carry

    send_bucket(0, 4)
    lax.fori_loop(6, H, local_step, 0)
    wait_rows(1, 0)
    before = jnp.where(odd == 1, 1.0, 0.0) * yr[jnp.maximum(y - 1, 0)].astype(F32)
    b1_send[0] = (level_factor(2 * odd, 1) * before).astype(BF16)
    b1_send[1] = (level_factor(2 * odd + 1, 1) * (before + own_f[0])).astype(BF16)
    send_bucket(1, 0)
    send_bucket(1, 4)
    buckets[1, z] = b1_send[z // 4]

    lax.fori_loop(2, NY, wait_rows, 0)
    earlier = jnp.zeros((DK, DK), F32)
    plane = jnp.zeros((DK, DK), F32)
    for yy in range(NY):
        r = yr[yy].astype(F32)
        plane = plane + r
        earlier = earlier + jnp.where(yy < 2 * pair, 1.0, 0.0) * r
    xt[x] = plane.astype(BF16)
    for xx in range(1, NX):

        @pl.when(xx > x)
        def _():
            plane_copy(x, xx).start()

    b1_send[2] = (level_factor(pair, 2) * earlier).astype(BF16)
    send_bucket(2, 0)
    buckets[2, z] = b1_send[2]

    plane_f[...] = jnp.zeros((DK, DK), F32)
    for xx in range(NX - 1):

        @pl.when(xx < x)
        def _():
            plane_copy(xx, xx).wait_recv()
            plane_f[...] += xt[xx].astype(F32)

    b1_send[3] = (level_factor(x, 3) * plane_f[...]).astype(BF16)
    send_bucket(3, 0)
    send_bucket(2, 4)
    send_bucket(3, 4)
    buckets[3, z] = b1_send[3]

    def wait_bucket(level, head):
        @pl.when(head != z)
        def _():
            bucket_copy(level, b1_send.at[3], head, head).wait_recv()

    def project(level, head):
        return weight(head, level + 1) * jnp.dot(qs[head], buckets[level, head], preferred_element_type=F32)

    def wait_level(level, first):
        def step(head, carry):
            wait_bucket(level, head)
            return carry

        @pl.when(needs(level, z))
        def _():
            lax.fori_loop(first, first + 4, step, 0)

    def add_level(level):
        @pl.when(needs(level, z))
        def _():
            for first in (0, 4):
                wait_level(level, first)
                for head in range(first, first + 4):
                    acc[head] += project(level, head)

    def store(head):
        cols = pl.ds(head * DK, DK)
        return pltpu.make_async_copy(obuf.at[head], out_hbm.at[:, cols], out_sem.at[head])

    def clear(level):
        @pl.when(jnp.logical_not(needs(level, z)))
        def _():
            for head in range(H):
                buckets[level, head] = jnp.zeros((DK, DK), BF16)

    clear(2)
    clear(3)
    add_level(0)
    add_level(1)
    for first in (0, 4):
        wait_level(2, first)
        wait_level(3, first)
        for head in range(first, first + 4):
            mixed = acc[head] + project(2, head) + project(3, head)
            mean = jnp.sum(mixed * mixed, axis=-1, keepdims=True) * (1.0 / DK)
            gain = gain_ref[:, head * DK : (head + 1) * DK]
            obuf[head] = (mixed * lax.rsqrt(mean + EPS) * gain).astype(BF16)
            store(head).start()

    def drain(step, carry):
        to = lax.rem(z + step, NZ)
        from_row(to).wait_send()
        row_copy(y, lax.rem(y + step, NY)).wait_send()
        for level in range(4):

            @pl.when(needs(level, to))
            def _():
                bucket_copy(level, b1_send.at[3], to, z).wait_send()

        return carry

    lax.fori_loop(1, NZ, drain, 0)
    for xx in range(1, NX):

        @pl.when(xx > x)
        def _():
            plane_copy(x, xx).wait_send()

    for head in range(H):
        store(head).wait()


def shards(query_in, key_in, value_in, conv_weight, level_weights, out_gain):
    hbm = pl.BlockSpec(memory_space=pltpu.HBM)
    dma = pltpu.SemaphoreType.DMA
    return pl.pallas_call(
        kernel,
        out_shape=jax.ShapeDtypeStruct((T, H * DK), BF16),
        in_specs=[hbm] * 6,
        out_specs=hbm,
        scratch_shapes=[
            pltpu.VMEM((3, 4, H * DK), F32),
            pltpu.VMEM((5 * H, T), F32),
            pltpu.VMEM((1, H * DK), F32),
            pltpu.VMEM((3, H, T, DK), BF16),
            pltpu.VMEM((3, 16, H * DK), BF16),
            pltpu.VMEM((16, H * DK), F32),
            pltpu.VMEM((16, H * DK), BF16),
            pltpu.VMEM((16, H * DK), BF16),
            pltpu.VMEM((3, T + 8, DK), F32),
            pltpu.VMEM((2, H, 24, DK), F32),
            pltpu.VMEM((H, T, DK), BF16),
            pltpu.VMEM((H, T, DK), BF16),
            pltpu.VMEM((H, T, DK), BF16),
            pltpu.VMEM((H, T, DK), F32),
            pltpu.VMEM((H, T, DK), F32),
            pltpu.VMEM((H, DK, DK), BF16),
            pltpu.VMEM((NZ, DK, DK), BF16),
            pltpu.VMEM((NZ, DK, DK), BF16),
            pltpu.VMEM((4, DK, DK), BF16),
            pltpu.VMEM((NY, DK, DK), BF16),
            pltpu.VMEM((NX, DK, DK), BF16),
            pltpu.VMEM((4, H, DK, DK), BF16),
            pltpu.VMEM((H, T, DK), BF16),
            pltpu.VMEM((1, DK, DK), F32),
            pltpu.VMEM((DK, DK), F32),
            dma((3,)),
            dma((3, H)),
            dma((3,)),
            dma((H,)),
            dma((2,)),
            dma((NZ,)),
            dma((NZ,)),
            dma((NY,)),
            dma((NY,)),
            dma((NX,)),
            dma((NX,)),
            dma((4, NZ)),
            dma((4, NZ)),
        ],
        compiler_params=pltpu.CompilerParams(
            collective_id=0, has_side_effects=True, vmem_limit_bytes=60 * 1024 * 1024
        ),
        cost_estimate=pl.CostEstimate(flops=2 * 10**9, bytes_accessed=4 * 2**20, transcendentals=2 * 10**6),
    )(query_in, key_in, value_in, conv_weight, level_weights.reshape(5 * H, T), out_gain.reshape(1, H * DK))


def solution(mesh):
    return jax.shard_map(
        shards,
        mesh=mesh,
        in_specs=(
            P(("batch", "seq"), None),
            P(("batch", "seq"), None),
            P(("batch", "seq"), None),
            P(),
            P(None, None, ("batch", "seq")),
            P(),
        ),
        out_specs=P(("batch", "seq"), None),
        check_vma=False,
    )
```

```python
import functools

import jax
import jax.numpy as jnp
from jax import lax
from jax.experimental import pallas as pl
from jax.experimental.pallas import tpu as pltpu
from jax.sharding import PartitionSpec as P

MESH = pl.DeviceIdType.MESH
EPS = 1e-6
H = 8
DK = 128
T = 512
NX, NY, NZ = 4, 8, 8
F32 = jnp.float32
BF16 = jnp.bfloat16


def level_factor(digit, level):
    base = (1.0 / (T * 4.0**level)) ** 0.5
    return jnp.where(
        digit == 0, 0.0, jnp.where(digit == 1, base, jnp.where(digit == 2, base * 0.5**0.5, base * (1.0 / 3.0) ** 0.5))
    )


def kernel(
    q_hbm, k_hbm, v_hbm, cw_hbm, lw_hbm, gain_hbm, out_hbm,
    cw_ref, lw_ref, gain_ref,
    xin, tails, halo_f, halo_send, halo_recv, xf, xfs, qs, ks, vs, lwh, acc,
    state, a_recv, b0_send, b1_send, yr, xt, buckets, obuf, own_f, plane_f,
    par_sem, in_sem, tail_sem, out_sem, halo_sem, a_ss, a_rs, y_ss, y_rs, x_ss, x_rs, b_ss, b_rs,
):
    me = lax.axis_index("seq")
    core = lax.axis_index("batch")
    x, y, z = me // 64, lax.rem(me // 8, 8), lax.rem(me, 8)

    def dev(xx, yy, zz):
        return (xx * 64 + yy * 8 + zz, core)

    ins = (q_hbm, k_hbm, v_hbm)

    def head_of(step):
        return lax.rem(z + 1 + step, NZ)

    def load(stream, head):
        cols = pl.ds(pl.multiple_of(head * DK, DK), DK)
        return pltpu.make_async_copy(ins[stream].at[:, cols], xin.at[stream, head], in_sem.at[stream, head])

    def tail(stream):
        return pltpu.make_async_copy(ins[stream].at[pl.ds(T - 16, 16), :], tails.at[stream], tail_sem.at[stream])

    for stream in range(3):
        tail(stream).start()
    pars = [
        pltpu.make_async_copy(src, dst, par_sem.at[i])
        for i, (src, dst) in enumerate(((cw_hbm, cw_ref), (lw_hbm, lw_ref), (gain_hbm, gain_ref)))
    ]
    for copy in pars:
        copy.start()

    def start_loads(step, carry):
        for stream in (1, 2):
            load(stream, head_of(step)).start()
        return carry

    lax.fori_loop(0, H, start_loads, 0)

    def start_q(head, carry):
        load(0, head).start()
        return carry

    lax.fori_loop(0, H, start_q, 0)

    barrier = pltpu.get_barrier_semaphore()

    def greet_ring(step, carry):
        pl.semaphore_signal(barrier, inc=1, device_id=dev(x, y, lax.rem(z + step, NZ)), device_id_type=MESH)
        pl.semaphore_signal(barrier, inc=1, device_id=dev(x, lax.rem(y + step, NY), z), device_id_type=MESH)
        return carry

    lax.fori_loop(1, NZ, greet_ring, 0)
    for step in range(1, NX):
        pl.semaphore_signal(barrier, inc=1, device_id=dev(lax.rem(x + step, NX), y, z), device_id_type=MESH)
    pl.semaphore_signal(barrier, inc=1, device_id=(lax.rem(me + 255, 256), core), device_id_type=MESH)

    halo_f[...] = jnp.zeros_like(halo_f)
    for stream in range(3):
        tail(stream).wait()
        halo_f[pl.ds(3 * stream, 3), :] = tails[stream].astype(F32)[13:16, :]
    halo_send[...] = halo_f[...].astype(BF16)
    halo = pltpu.make_async_remote_copy(
        halo_send, halo_recv, halo_sem.at[0], halo_sem.at[1], device_id=(lax.rem(me + 1, 256), core), device_id_type=MESH
    )


    def taps(stream, head):
        cols = pl.ds(pl.multiple_of(head * DK, DK), DK)
        return [cw_ref[stream, pl.ds(j, 1), cols] for j in range(4)]

    def silu(c):
        return c * pl.reciprocal(1.0 + jnp.exp(-c), approx=True)

    def unit(a):
        return a * lax.rsqrt(jnp.sum(a * a, axis=-1, keepdims=True) + EPS)

    def conv_rows(src, w, row, count):
        c = w[0] * src[pl.ds(row + 5, count), :]
        for j in range(1, 4):
            c = c + w[j] * src[pl.ds(row + 5 + j, count), :]
        return silu(c)

    CH = 128

    def stream_head(stream, head, dst, halo_rows):
        w = taps(stream, head)
        buf = xf.at[stream]
        if halo_rows is None:
            buf[pl.ds(0, 8), :] = jnp.zeros((8, DK), F32)
        else:
            buf[pl.ds(5, 3), :] = halo_rows
        buf[pl.ds(8, T), :] = xin[stream, head].astype(F32)
        for row in range(0, T, CH):
            a = conv_rows(buf, w, row, CH)
            if stream < 2:
                a = unit(a)
            dst[head, pl.ds(row, CH), :] = a.astype(BF16)

    def kv_step(step, carry):
        head = head_of(step)
        for stream, dst in ((1, ks), (2, vs)):
            load(stream, head).wait()
            stream_head(stream, head, dst, None)
        return carry

    for copy in pars:
        copy.wait()
    ahead = jnp.where(z < 4, 4, 1)
    lax.fori_loop(0, ahead, kv_step, 0)
    pl.semaphore_wait(barrier, 18)
    halo.start()
    lax.fori_loop(ahead, H, kv_step, 0)

    halo.wait()
    halo_f[...] = jnp.where(me == 0, 0.0, halo_recv[...].astype(F32))

    def halo_rows(stream, head):
        cols = pl.ds(pl.multiple_of(head * DK, DK), DK)
        return halo_f[pl.ds(3 * stream, 3), cols]

    def to_owner(head):
        return pltpu.make_async_remote_copy(
            state.at[head], a_recv.at[z], a_ss.at[head], a_rs.at[z], device_id=dev(x, y, head), device_id_type=MESH
        )

    def from_row(source):
        return pltpu.make_async_remote_copy(
            state.at[source], a_recv.at[source], a_ss.at[source], a_rs.at[source],
            device_id=dev(x, y, source), device_id_type=MESH,
        )

    for stream, dst in ((1, ks), (2, vs)):
        for head in range(H):
            cols = slice(head * DK, (head + 1) * DK)
            xfs[stream - 1, head, pl.ds(5, 3), :] = halo_f[3 * stream : 3 * stream + 3, cols]
            xfs[stream - 1, head, pl.ds(8, 16), :] = xin[stream, head, pl.ds(0, 16), :].astype(F32)
    for stream, dst in ((1, ks), (2, vs)):
        for head in range(H):
            a = conv_rows(xfs.at[stream - 1, head], taps(stream, head), 0, 16)
            if stream == 1:
                a = unit(a)
            dst[head, pl.ds(0, 16), :] = a.astype(BF16)

    def state_of(head):
        return lax.dot_general(ks[head], vs[head], (((0,), (0,)), ((), ())), preferred_element_type=F32)

    def state_step(step, carry):
        head = head_of(step)
        state[head] = state_of(head).astype(BF16)
        to_owner(head).start()
        return carry

    lax.fori_loop(0, H - 1, state_step, 0)
    a_recv[z] = state_of(z).astype(BF16)

    lw = jnp.concatenate([lw_ref[...], jnp.zeros((128 - 5 * H, T), F32)], axis=0).T
    pos = lax.broadcasted_iota(jnp.int32, (T, 128), 0).astype(F32)
    lane = lax.broadcasted_iota(jnp.int32, (T, 128), 1)
    lw = jnp.where(lane < H, lw * lax.rsqrt(pos + 1.0), lw)
    for head in range(H):
        lwh[head] = lw if head == 0 else pltpu.roll(lw, 128 - head, 1)

    row_i = lax.broadcasted_iota(jnp.int32, (256, 256), 0)
    col_i = lax.broadcasted_iota(jnp.int32, (256, 256), 1)
    causal = row_i >= col_i
    NT = (((1,), (1,)), ((), ()))

    def weight(head, level):
        return jnp.broadcast_to(lwh[head, :, pl.ds(8 * level, 1)], (T, DK))

    def local_step(head, carry):
        load(0, head).wait()
        stream_head(0, head, qs, halo_rows(0, head))
        q0, q1 = qs[head, pl.ds(0, 256), :], qs[head, pl.ds(256, 256), :]
        k0, k1 = ks[head, pl.ds(0, 256), :], ks[head, pl.ds(256, 256), :]
        v0, v1 = vs[head, pl.ds(0, 256), :], vs[head, pl.ds(256, 256), :]
        s00 = jnp.where(causal, lax.dot_general(q0, k0, NT, preferred_element_type=F32), 0.0).astype(BF16)
        s10 = lax.dot_general(q1, k0, NT, preferred_element_type=F32).astype(BF16)
        s11 = jnp.where(causal, lax.dot_general(q1, k1, NT, preferred_element_type=F32), 0.0).astype(BF16)
        o0 = jnp.dot(s00, v0, preferred_element_type=F32)
        o1 = jnp.dot(s10, v0, preferred_element_type=F32) + jnp.dot(s11, v1, preferred_element_type=F32)
        w = weight(head, 0)
        acc[head, pl.ds(0, 256), :] = w[:256] * o0
        acc[head, pl.ds(256, 256), :] = w[256:] * o1
        return carry

    def from_group(first):
        def wait(source, carry):
            @pl.when(source != z)
            def _():
                from_row(source).wait_recv()

            return carry

        lax.fori_loop(first, first + 4, wait, 0)

    def group_sum(first):
        group = a_recv[first].astype(F32)
        for digit in range(1, 4):
            b0_send[first + digit] = (group * ((1.0 / (T * digit)) ** 0.5)).astype(BF16)
            group = group + a_recv[first + digit].astype(F32)
        return group

    odd = lax.rem(y, 2)
    pair = y // 2

    def needs(level, zz):
        return (lax.rem(zz, 4) != 0, (zz >= 4) | (odd == 1), pair > 0, x > 0)[level]

    def bucket_copy(level, src, to, head):
        return pltpu.make_async_remote_copy(
            src, buckets.at[level, head], b_ss.at[level, to], b_rs.at[level, head], device_id=dev(x, y, to), device_id_type=MESH
        )

    def sent(level, to):
        if level == 0:
            return b0_send.at[to]
        return b1_send.at[to // 4 if level == 1 else level]

    def send_bucket(level, first):
        def step(to, carry):
            @pl.when((to != z) & needs(level, to))
            def _():
                bucket_copy(level, sent(level, to), to, z).start()

            return carry

        lax.fori_loop(first, first + 4, step, 0)

    def row_copy(src_y, dst_y):
        return pltpu.make_async_remote_copy(
            yr.at[src_y], yr.at[src_y], y_ss.at[dst_y], y_rs.at[src_y], device_id=dev(x, dst_y, z), device_id_type=MESH
        )

    def plane_copy(src_x, dst_x):
        return pltpu.make_async_remote_copy(
            xt.at[src_x], xt.at[src_x], x_ss.at[dst_x], x_rs.at[src_x], device_id=dev(dst_x, y, z), device_id_type=MESH
        )

    lax.fori_loop(0, 3, local_step, 0)
    from_group(0)
    own_f[0] = group_sum(0)
    send_bucket(0, 0)
    lax.fori_loop(3, 6, local_step, 0)

    from_group(4)
    yr[y] = (own_f[0] + group_sum(4)).astype(BF16)

    for step in (1, 4, 5, 3, 6, 2, 7):
        row_copy(y, lax.rem(y + step, NY)).start()

    @pl.when(needs(0, z))
    def _():
        buckets[0, z] = b0_send[z]


    def wait_rows(step, carry):
        src = lax.rem(y + NY - step, NY)
        row_copy(src, src).wait_recv()
        return carry

    send_bucket(0, 4)
    lax.fori_loop(6, H, local_step, 0)
    wait_rows(1, 0)
    before = jnp.where(odd == 1, 1.0, 0.0) * yr[jnp.maximum(y - 1, 0)].astype(F32)
    b1_send[0] = (level_factor(2 * odd, 1) * before).astype(BF16)
    b1_send[1] = (level_factor(2 * odd + 1, 1) * (before + own_f[0])).astype(BF16)
    send_bucket(1, 0)
    send_bucket(1, 4)
    buckets[1, z] = b1_send[z // 4]

    lax.fori_loop(2, NY, wait_rows, 0)
    earlier = jnp.zeros((DK, DK), F32)
    plane = jnp.zeros((DK, DK), F32)
    for yy in range(NY):
        r = yr[yy].astype(F32)
        plane = plane + r
        earlier = earlier + jnp.where(yy < 2 * pair, 1.0, 0.0) * r
    xt[x] = plane.astype(BF16)
    for xx in range(1, NX):

        @pl.when(xx > x)
        def _():
            plane_copy(x, xx).start()

    b1_send[2] = (level_factor(pair, 2) * earlier).astype(BF16)
    send_bucket(2, 0)
    buckets[2, z] = b1_send[2]

    plane_f[...] = jnp.zeros((DK, DK), F32)
    for xx in range(NX - 1):

        @pl.when(xx < x)
        def _():
            plane_copy(xx, xx).wait_recv()
            plane_f[...] += xt[xx].astype(F32)

    b1_send[3] = (level_factor(x, 3) * plane_f[...]).astype(BF16)
    send_bucket(3, 0)
    send_bucket(2, 4)
    send_bucket(3, 4)
    buckets[3, z] = b1_send[3]

    def wait_bucket(level, head):
        @pl.when(head != z)
        def _():
            bucket_copy(level, b1_send.at[3], head, head).wait_recv()

    def project(level, head):
        return weight(head, level + 1) * jnp.dot(qs[head], buckets[level, head], preferred_element_type=F32)

    def wait_level(level, first):
        def step(head, carry):
            wait_bucket(level, head)
            return carry

        @pl.when(needs(level, z))
        def _():
            lax.fori_loop(first, first + 4, step, 0)

    def add_level(level):
        @pl.when(needs(level, z))
        def _():
            for first in (0, 4):
                wait_level(level, first)
                for head in range(first, first + 4):
                    acc[head] += project(level, head)

    def store(head):
        cols = pl.ds(head * DK, DK)
        return pltpu.make_async_copy(obuf.at[head], out_hbm.at[:, cols], out_sem.at[head])

    def clear(level):
        @pl.when(jnp.logical_not(needs(level, z)))
        def _():
            for head in range(H):
                buckets[level, head] = jnp.zeros((DK, DK), BF16)

    clear(2)
    clear(3)
    add_level(0)
    add_level(1)
    for first in (0, 4):
        wait_level(2, first)
        wait_level(3, first)
        for head in range(first, first + 4):
            mixed = acc[head] + project(2, head) + project(3, head)
            mean = jnp.sum(mixed * mixed, axis=-1, keepdims=True) * (1.0 / DK)
            gain = gain_ref[:, head * DK : (head + 1) * DK]
            obuf[head] = (mixed * lax.rsqrt(mean + EPS) * gain).astype(BF16)
            store(head).start()

    def drain(step, carry):
        to = lax.rem(z + step, NZ)
        from_row(to).wait_send()
        row_copy(y, lax.rem(y + step, NY)).wait_send()
        for level in range(4):

            @pl.when(needs(level, to))
            def _():
                bucket_copy(level, b1_send.at[3], to, z).wait_send()

        return carry

    lax.fori_loop(1, NZ, drain, 0)
    for xx in range(1, NX):

        @pl.when(xx > x)
        def _():
            plane_copy(x, xx).wait_send()

    for head in range(H):
        store(head).wait()


def shards(query_in, key_in, value_in, conv_weight, level_weights, out_gain):
    hbm = pl.BlockSpec(memory_space=pltpu.HBM)
    dma = pltpu.SemaphoreType.DMA
    return pl.pallas_call(
        kernel,
        out_shape=jax.ShapeDtypeStruct((T, H * DK), BF16),
        in_specs=[hbm] * 6,
        out_specs=hbm,
        scratch_shapes=[
            pltpu.VMEM((3, 4, H * DK), F32),
            pltpu.VMEM((5 * H, T), F32),
            pltpu.VMEM((1, H * DK), F32),
            pltpu.VMEM((3, H, T, DK), BF16),
            pltpu.VMEM((3, 16, H * DK), BF16),
            pltpu.VMEM((16, H * DK), F32),
            pltpu.VMEM((16, H * DK), BF16),
            pltpu.VMEM((16, H * DK), BF16),
            pltpu.VMEM((3, T + 8, DK), F32),
            pltpu.VMEM((2, H, 24, DK), F32),
            pltpu.VMEM((H, T, DK), BF16),
            pltpu.VMEM((H, T, DK), BF16),
            pltpu.VMEM((H, T, DK), BF16),
            pltpu.VMEM((H, T, DK), F32),
            pltpu.VMEM((H, T, DK), F32),
            pltpu.VMEM((H, DK, DK), BF16),
            pltpu.VMEM((NZ, DK, DK), BF16),
            pltpu.VMEM((NZ, DK, DK), BF16),
            pltpu.VMEM((4, DK, DK), BF16),
            pltpu.VMEM((NY, DK, DK), BF16),
            pltpu.VMEM((NX, DK, DK), BF16),
            pltpu.VMEM((4, H, DK, DK), BF16),
            pltpu.VMEM((H, T, DK), BF16),
            pltpu.VMEM((1, DK, DK), F32),
            pltpu.VMEM((DK, DK), F32),
            dma((3,)),
            dma((3, H)),
            dma((3,)),
            dma((H,)),
            dma((2,)),
            dma((NZ,)),
            dma((NZ,)),
            dma((NY,)),
            dma((NY,)),
            dma((NX,)),
            dma((NX,)),
            dma((4, NZ)),
            dma((4, NZ)),
        ],
        compiler_params=pltpu.CompilerParams(
            collective_id=0, has_side_effects=True, vmem_limit_bytes=60 * 1024 * 1024
        ),
        cost_estimate=pl.CostEstimate(flops=2 * 10**9, bytes_accessed=4 * 2**20, transcendentals=2 * 10**6),
    )(query_in, key_in, value_in, conv_weight, level_weights.reshape(5 * H, T), out_gain.reshape(1, H * DK))


def solution(mesh):
    return jax.shard_map(
        shards,
        mesh=mesh,
        in_specs=(
            P(("batch", "seq"), None),
            P(("batch", "seq"), None),
            P(("batch", "seq"), None),
            P(),
            P(None, None, ("batch", "seq")),
            P(),
        ),
        out_specs=P(("batch", "seq"), None),
        check_vma=False,
    )
```
